32 devices in a mesh: gx: 8 (over z, y), gy: 4 (over x, core).
Axes of the slice: x: 2, y: 2, z: 4, core: 2. Of those that a mesh axis runs over, the one named last changes fastest.
Arguments:
- modes_start: float32 [16, 64, 2048], P(None, 'gx', 'gy'), may hold values from -6 to 6
- search_start: float32 [16, 64, 2048], P(None, 'gx', 'gy'), may hold values from -6 to 6
- stiffness: float32 [64, 2048], P('gx', 'gy'), may hold values from 1 to 10
- density: float32 [64, 2048], P('gx', 'gy'), may hold values from 0.3 to 3
Outputs:
- modes: float32 [16, 64, 2048], P(None, 'gx', 'gy')
- search: float32 [16, 64, 2048], P(None, 'gx', 'gy')
- ritz: float32 [16], replicated
The draws below stay inside these ranges and needn't reach their ends.
All inputs are finite; a program needn't handle non-finite values.
Results may differ from the reference program's by a relative error of at most 0.00018.
Values sent between devices are 32-bit elements; how exact they have to be, the bound alone decides.
A program may use at most 64 MiB of HBM per device.

```python
import math
import jax
import jax.numpy as jnp
from jax import lax

NZ = 16
MODES = 16
ITERS = 2
INNER = 6
NX = 64
NY = 128


def common_normal(key):
    return jnp.clip(jax.random.normal(key, (MODES, NX, NY * NZ), jnp.float32), -6.0, 6.0)


def draw_modes_start(key, part):
    return common_normal(key)


def draw_search_start(key, part):
    shared = common_normal(key)
    key = jax.random.fold_in(key, 7)
    return jnp.clip(0.6 * shared + 0.8 * common_normal(key), -6.0, 6.0)


def steps_of(own_key, extent, split, smallest, top_value):
    factor_of = 1.0
    for dim, blocks in split:
        steps = jax.random.uniform(jax.random.fold_in(jax.random.fold_in(own_key, 6), dim), (blocks,), jnp.float32, smallest / len(split), top_value / len(split))
        factor_of = factor_of * jnp.repeat(jnp.exp(steps), extent[dim] // blocks).reshape((-1,) + (1,) * (len(extent) - 1 - dim))
    return factor_of


def setup_inputs(seed: int = 0) -> dict:
    keys = jax.random.split(jax.random.key(seed), 5)
    modes_start = draw_modes_start(jax.random.fold_in(keys[4], 71), 0)
    search_start = draw_search_start(jax.random.fold_in(keys[4], 71), 0)
    stiffness = jnp.clip(jnp.exp(math.log(10.0) - 2.3025851 * jax.random.uniform(keys[2], (NX, NY * NZ), jnp.float32) ** steps_of(keys[2], (NX, NY * NZ), ((0, 8), (1, 4)), -0.2, 0.2)), 1.0, 10.0)
    density = jnp.clip(jnp.exp(math.log(3.0) - 2.3025851 * jax.random.uniform(keys[3], (NX, NY * NZ), jnp.float32) ** steps_of(keys[3], (NX, NY * NZ), ((0, 8), (1, 4)), -0.2, 0.2)), 0.3, 3.0)
    return {"modes_start": modes_start, "search_start": search_start, "stiffness": stiffness, "density": density}


SHIFTS = [(first, second, third) for first in (-1, 0, 1) for second in (-1, 0, 1) for third in (-1, 0, 1)]

def stiff_weight(shift):
    nonzero = sum((1 for value in shift if value != 0))
    return 1.0 / 2 ** (nonzero - 1)

def mass_weight(shift):
    product = 1.0
    for value in shift:
        product = product * (4.0 / 6.0 if value == 0 else 1.0 / 6.0)
    return product

def solve_lower(lower, right):
    return lax.linalg.triangular_solve(lower, right, left_side=True, lower=True)

def solve_upper_t(lower, right):
    return lax.linalg.triangular_solve(lower, right, left_side=True, lower=True, transpose_a=True)

def project(lower, matrix):
    first_half = solve_lower(lower, matrix)
    second_half = solve_lower(lower, first_half.T)
    return 0.5 * (second_half + second_half.T)

def small_problem(lower_gram, stiff_gram, mass_gram):
    proj_stiff = project(lower_gram, stiff_gram)
    proj_mass = project(lower_gram, mass_gram)
    lower_stiff = jnp.linalg.cholesky(proj_stiff)
    block_width = proj_stiff.shape[0]
    columns = jnp.eye(block_width, MODES, dtype=jnp.float32)
    for inner_index in range(INNER):
        moved = jnp.dot(proj_mass, columns, precision=lax.Precision.HIGHEST)
        solved = solve_upper_t(lower_stiff, solve_lower(lower_stiff, moved))
        correlation = jnp.dot(solved.T, jnp.dot(proj_mass, solved, precision=lax.Precision.HIGHEST), precision=lax.Precision.HIGHEST)
        correlation = 0.5 * (correlation + correlation.T)
        lower_correlation = jnp.linalg.cholesky(correlation)
        columns = solve_lower(lower_correlation, solved.T).T
    ritz_values = lax.optimization_barrier(jnp.sum(columns * jnp.dot(proj_stiff, columns, precision=lax.Precision.HIGHEST), axis=0))
    trimmed = jnp.concatenate([jnp.zeros((MODES, MODES), jnp.float32), columns[MODES:]], axis=0)
    return (solve_upper_t(lower_gram, columns), solve_upper_t(lower_gram, trimmed), ritz_values)

def take_tap(padded, shift):
    first, second, third = shift
    return padded[1 + first:1 + first + NX, 1 + second:1 + second + NY, 1 + third:1 + third + NZ]

def column_ops(field, stiff_grid, root_grid):
    padded = jnp.pad(field, 1)
    stiff_pad = jnp.pad(stiff_grid, 1)
    scaled_pad = jnp.pad(root_grid * field, 1)
    stiff_out = jnp.zeros_like(field)
    mass_sum = jnp.zeros_like(field)
    for shift in SHIFTS:
        if shift != (0, 0, 0):
            stiff_out = stiff_out + stiff_weight(shift) * 0.5 * (stiff_grid + take_tap(stiff_pad, shift)) * (field - take_tap(padded, shift))
        mass_sum = mass_sum + mass_weight(shift) * take_tap(scaled_pad, shift)
    return (stiff_out, root_grid * mass_sum)

def apply_block(block, stiff_grid, root_grid):

    def one_column(column):
        stiff_out, mass_out = column_ops(column.reshape(NX, NY, NZ), stiff_grid, root_grid)
        return (stiff_out.reshape(-1), mass_out.reshape(-1))
    return lax.map(one_column, block)

def reference(modes_start, search_start, stiffness, density):
    stiff_grid = stiffness.reshape(NX, NY, NZ)
    root_grid = jnp.sqrt(density).reshape(NX, NY, NZ)
    current = modes_start.reshape(MODES, -1)
    search = search_start.reshape(MODES, -1)
    ritz_values = jnp.zeros((MODES,), jnp.float32)
    for iteration in range(ITERS):
        stiff_modes, mass_modes = apply_block(current, stiff_grid, root_grid)
        quotient = lax.optimization_barrier(jnp.sum(current * stiff_modes, axis=1)) / lax.optimization_barrier(jnp.sum(current * mass_modes, axis=1))
        residual = stiff_modes - mass_modes * quotient[:, None]
        stiff_rest, mass_rest = apply_block(jnp.concatenate([residual, search], axis=0), stiff_grid, root_grid)
        wide = jnp.concatenate([current, residual, search], axis=0)
        stiff_wide = jnp.concatenate([stiff_modes, stiff_rest], axis=0)
        mass_wide = jnp.concatenate([mass_modes, mass_rest], axis=0)
        gram_matrix = jnp.dot(wide, wide.T, precision=lax.Precision.HIGHEST)
        stiff_gram = jnp.dot(wide, stiff_wide.T, precision=lax.Precision.HIGHEST)
        mass_gram = jnp.dot(wide, mass_wide.T, precision=lax.Precision.HIGHEST)
        lower_gram = jnp.linalg.cholesky(gram_matrix)
        coef_modes, coef_search, ritz_values = small_problem(lower_gram, stiff_gram, mass_gram)
        current = jnp.dot(coef_modes.T, wide, precision=lax.Precision.HIGHEST)
        search = jnp.dot(coef_search.T, wide, precision=lax.Precision.HIGHEST)
    scale_factor = math.sqrt(NX * NY * NZ)
    modes_out = (current * scale_factor).reshape(MODES, NX, NY * NZ)
    search_out = (search * scale_factor).reshape(MODES, NX, NY * NZ)
    return (modes_out, search_out, ritz_values)
```

```python
import functools
import math

import jax
import jax.numpy as jnp
from jax import lax
from jax.experimental import pallas as pl
from jax.experimental.pallas import tpu as pltpu
from jax.sharding import PartitionSpec as P

NZ = 16
MODES = 16
POWERS = (2, 2, 1, 1)
MESH = pl.DeviceIdType.MESH
F32 = jnp.float32
HIGHEST = lax.Precision.HIGHEST
WIDE = 3 * MODES
COEF, XLO, PLO, RLO, R2LO, TOP = 0, 8, 24, 40, 56, 72


def dot_nt(left, right):
    return lax.dot_general(left, right, (((1,), (1,)), ((), ())), precision=HIGHEST,
                           preferred_element_type=F32)


def dot_nn(left, right):
    return lax.dot_general(left, right, (((1,), (0,)), ((), ())), precision=HIGHEST,
                           preferred_element_type=F32)


def iota(shape, dim):
    return lax.broadcasted_iota(jnp.int32, shape, dim)


def jordan_step(table, k):
    rows = table.shape[0]
    pivot_row = table[k:k + 1, :] * (1.0 / table[k:k + 1, k:k + 1])
    return jnp.where(iota((rows, 1), 0) == k, pivot_row, table - table[:, k:k + 1] * pivot_row)


def orthonormal(gram, rows_t):
    count = gram.shape[0]
    row_id = iota((count, 1), 0)
    for k in range(count - 1):
        factor = jnp.where(row_id > k, gram[:, k:k + 1] * (1.0 / gram[k:k + 1, k:k + 1]), 0.0)
        gram, rows_t = gram - factor * gram[k:k + 1, :], rows_t - factor * rows_t[k:k + 1, :]
    diag = jnp.sum(jnp.where(iota(gram.shape, 0) == iota(gram.shape, 1), gram, 0.0),
                   axis=1, keepdims=True)
    return rows_t * lax.rsqrt(diag)


def small_problem(table):
    stiff = table[:, 0:WIDE]
    mass = table[:, WIDE:2 * WIDE]
    cross = table[:, 2 * WIDE:2 * WIDE + MODES]
    solved = table
    corner = jnp.concatenate(
        [cross[0:MODES], (iota((MODES, MODES), 0) == iota((MODES, MODES), 1)).astype(F32)], axis=1)
    for k in range(WIDE):
        solved = jordan_step(solved, k)
        if k < MODES:
            corner = jordan_step(corner, k)
    step = solved[:, WIDE:2 * WIDE]
    coef_t = (iota((MODES, WIDE), 0) == iota((MODES, WIDE), 1)).astype(F32)
    for power in POWERS:
        for _ in range(power):
            coef_t = dot_nt(coef_t, step)
        coef_t = orthonormal(dot_nt(dot_nn(coef_t, mass), coef_t), coef_t)
    ritz = jnp.sum(dot_nn(coef_t, stiff) * coef_t, axis=1, keepdims=True)
    norm = jnp.sum(dot_nn(coef_t, mass) * coef_t, axis=1, keepdims=True)
    rest_t = jnp.where(iota((MODES, WIDE), 1) >= MODES, coef_t, 0.0)
    top = dot_nn(dot_nn(rest_t, cross), corner[:, MODES:2 * MODES])
    search_t = rest_t - jnp.concatenate([top, jnp.zeros((MODES, WIDE - MODES), F32)], axis=1)
    return coef_t, search_t, ritz, ritz / norm


def kernel(ngx, ngy, x_ref, p_ref, s_ref, d_ref, xo_ref, po_ref, rz_ref,
           ext, w2, q, k0, pk, side, th_x, th_y, gr_x, gr_y,
           h_send, h_recv, th_xs, th_xr, th_ys, th_yr, gr_xs, gr_xr, gr_ys, gr_yr):
    rows, lanes = s_ref.shape
    full = lanes + 128
    gx, gy = lax.axis_index("gx"), lax.axis_index("gy")
    lane_id = iota((1, full), 1)
    depth = lane_id % NZ
    low = (depth >= 1).astype(F32)
    high = (depth <= NZ - 2).astype(F32)
    tile_id = iota((1, 128), 1)

    barrier = pltpu.get_barrier_semaphore()
    for o in range(1, ngx):
        pl.semaphore_signal(barrier, inc=1, device_id=(lax.rem(gx + o, ngx), gy), device_id_type=MESH)
    for o in range(1, ngy):
        pl.semaphore_signal(barrier, inc=1, device_id=(gx, lax.rem(gy + o, ngy)), device_id_type=MESH)

    def exists(dx, dy):
        good = None
        for cond in ([gx > 0] if dx < 0 else [gx < ngx - 1] if dx > 0 else []) + (
                [gy > 0] if dy < 0 else [gy < ngy - 1] if dy > 0 else []):
            good = cond if good is None else jnp.logical_and(good, cond)
        return good

    for dx in (1, ngx - 1):
        for dy in (1, ngy - 1):
            pl.semaphore_signal(barrier, inc=1, device_id_type=MESH,
                                device_id=(lax.rem(gx + dx, ngx), lax.rem(gy + dy, ngy)))
    pl.semaphore_wait(barrier, ngx - 1 + ngy - 1 + 4)

    for r in range(rows):
        ext[r + 1, XLO:PLO, 0:lanes] = x_ref[:, r, :]
        ext[r + 1, PLO:RLO, 0:lanes] = p_ref[:, r, :]
        ext[r + 1, COEF:COEF + 8, 0:lanes] = jnp.concatenate(
            [s_ref[r:r + 1, :], jnp.sqrt(d_ref[r:r + 1, :]), jnp.zeros((6, lanes), F32)], axis=0)
        q[r, 2 * WIDE:2 * WIDE + MODES, :] = x_ref[:, r, :]

    steps = [(dx, dy) for dx in (-1, 0, 1) for dy in (-1, 0, 1) if (dx, dy) != (0, 0)]

    def exchange(phase, lo, hi):
        left = jnp.zeros((hi - lo, 128), F32)
        right = jnp.zeros((hi - lo, 128), F32)
        for r in range(rows):
            here = jnp.logical_and(tile_id >= NZ * r, tile_id < NZ * (r + 1))
            first = ext[r + 1, lo:hi, 0:128]
            last = pltpu.roll(ext[r + 1, lo:hi, lanes - 128:lanes], NZ, 1)
            if r:
                first, last = pltpu.roll(first, NZ * r, 1), pltpu.roll(last, NZ * r, 1)
            left, right = jnp.where(here, first, left), jnp.where(here, last, right)
        pk[0, lo:hi, :] = left
        pk[1, lo:hi, :] = right
        copies = []
        for i, (dx, dy) in enumerate(steps):
            back = steps.index((-dx, -dy))
            if dy == 0:
                src = ext.at[1 if dx < 0 else rows, lo:hi, 0:lanes]
                dst = ext.at[rows + 1 if dx < 0 else 0, lo:hi, 0:lanes]
            else:
                src = pk.at[0 if dy < 0 else 1, lo:hi]
                dst = side.at[back, lo:hi]
            copy = pltpu.make_async_remote_copy(
                src_ref=src, dst_ref=dst, send_sem=h_send.at[phase, i], recv_sem=h_recv.at[phase, back],
                device_id=(gx + dx, gy + dy), device_id_type=MESH)
            copies.append(copy)
            there = exists(dx, dy)

            @pl.when(there)
            def _(copy=copy):
                copy.start()

            @pl.when(jnp.logical_not(there))
            def _(i=i, dx=dx, dy=dy):
                if dy == 0:
                    ext[0 if dx < 0 else rows + 1, lo:hi, 0:lanes] = jnp.zeros((hi - lo, lanes), F32)
                else:
                    side[i, lo:hi, :] = jnp.zeros((hi - lo, 128), F32)
        for i, (dx, dy) in enumerate(steps):
            back = steps.index((-dx, -dy))

            @pl.when(exists(dx, dy))
            def _(i=i, back=back):
                copies[i].wait_send()
                copies[back].wait_recv()
        for e in range(rows + 2):
            dx, r = (-1, rows - 1) if e == 0 else (1, 0) if e == rows + 1 else (0, e - 1)
            from_left = side[steps.index((dx, -1)), lo:hi, :]
            from_right = side[steps.index((dx, 1)), lo:hi, :]
            from_left = pltpu.roll(from_left, (112 - NZ * r) % 128, 1) if (112 - NZ * r) % 128 else from_left
            from_right = pltpu.roll(from_right, (128 - NZ * r) % 128, 1) if r else from_right
            ext[e, lo:hi, lanes:full] = jnp.where(
                tile_id < NZ, from_right, jnp.where(tile_id >= 128 - NZ, from_left, 0.0))

    def reduce_line(size, me, place, value, slots, send, recv):
        slots[me] = value
        copies = []
        for o in range(1, size):
            copy = pltpu.make_async_remote_copy(
                src_ref=slots.at[me], dst_ref=slots.at[me], send_sem=send.at[o], recv_sem=recv.at[o],
                device_id=place(lax.rem(me + o, size)), device_id_type=MESH)
            copy.start()
            copies.append(copy)
        for copy in copies:
            copy.wait()
        total = slots[0]
        for o in range(1, size):
            total = total + slots[o]
        return total

    def all_reduce(value, sx, sy, xs, xr, ys, yr):
        value = reduce_line(ngx, gx, lambda other: (other, gy), value, sx, xs, xr)
        return reduce_line(ngy, gy, lambda other: (gx, other), value, sy, ys, yr)

    def plane(value, center, edge):
        if center == 1.0:
            value = value + edge * (pltpu.roll(value, 1, 1) * low + pltpu.roll(value, full - 1, 1) * high)
            return value + edge * (pltpu.roll(value, NZ, 1) + pltpu.roll(value, full - NZ, 1))
        value = center * value + (pltpu.roll(value, 1, 1) * low + pltpu.roll(value, full - 1, 1) * high)
        return center * value + (pltpu.roll(value, NZ, 1) + pltpu.roll(value, full - NZ, 1))

    def operators(r, lo):
        before, here, after = [ext[r + j, lo:lo + MODES, :] for j in range(3)]
        s_b, s_h, s_a = [ext[r + j, 0:1, :] for j in range(3)]
        d_b, d_h, d_a = [ext[r + j, 1:2, :] for j in range(3)]
        plain = plane(here + 0.5 * (before + after), 1.0, 0.5)
        stiff = plane(s_h * here + 0.5 * (s_b * before + s_a * after), 1.0, 0.5)
        mass = plane(4.0 * (d_h * here) + (d_b * before + d_a * after), 4.0, 1.0)
        field = here[:, 0:lanes]
        k_out = field * k0[r, 0:1, :] - s_h[:, 0:lanes] * plain[:, 0:lanes] - stiff[:, 0:lanes]
        m_out = (d_h[:, 0:lanes] * (1.0 / 216.0)) * mass[:, 0:lanes]
        return field, k_out, m_out

    exchange(0, COEF, RLO)

    def coef_row(r, carry):
        before, here, after = [ext[r + j, 0:8, :] for j in range(3)]
        near = plane(here + 0.5 * (before + after), 1.0, 0.5)
        k0[r] = 8.0 * here[:, 0:lanes] + near[:, 0:lanes]
        return carry

    lax.fori_loop(0, rows, coef_row, 0)

    def fold(value):
        total = value[:, 0:128]
        for j in range(1, lanes // 128):
            total = total + value[:, 128 * j:128 * (j + 1)]
        return total

    def mode_row(r, carry):
        field, k_out, m_out = operators(r, XLO)
        q[r, 0:MODES, :] = k_out
        q[r, WIDE:WIDE + MODES, :] = m_out
        return carry[0] + fold(field * k_out), carry[1] + fold(field * m_out)

    zero = jnp.zeros((MODES, 128), F32)
    numer, denom = lax.fori_loop(0, rows, mode_row, (zero, zero))
    sums = all_reduce(jnp.concatenate([numer, denom], axis=0), th_x, th_y, th_xs, th_xr, th_ys, th_yr)
    sums = jnp.sum(sums, axis=1, keepdims=True)
    theta = sums[0:MODES] / sums[MODES:2 * MODES]

    def residual_row(r, carry):
        ext[r + 1, RLO:R2LO, 0:lanes] = q[r, 0:MODES, :] - q[r, WIDE:WIDE + MODES, :] * theta
        return carry

    lax.fori_loop(0, rows, residual_row, 0)
    exchange(1, RLO, R2LO)

    def rest_row(r, total):
        _, k_out, m_out = operators(r, PLO)
        q[r, MODES:2 * MODES, :] = k_out
        q[r, WIDE + MODES:WIDE + 2 * MODES, :] = m_out
        _, k_out, m_out = operators(r, RLO)
        q[r, 2 * MODES:WIDE, :] = k_out
        q[r, WIDE + 2 * MODES:2 * WIDE, :] = m_out
        return total + dot_nt(ext[r + 1, XLO:R2LO, 0:lanes], q[r])

    q_pad = q.shape[1] - 2 * WIDE - MODES
    for r in range(rows):
        q[r, 2 * WIDE + MODES:, :] = jnp.zeros((q_pad, lanes), F32)
    table = lax.fori_loop(0, rows, rest_row, jnp.zeros((WIDE, 128), F32))
    table = all_reduce(table, gr_x.at[0], gr_y.at[0], gr_xs.at[0], gr_xr.at[0], gr_ys.at[0], gr_yr.at[0])
    coef_t, search_t, _, theta2 = small_problem(table)
    both = jnp.concatenate([coef_t, search_t], axis=0)

    def move_row(r, carry):
        new = dot_nn(both, ext[r + 1, XLO:R2LO, 0:lanes])
        new_k = dot_nn(both, q[r, 0:WIDE, :])
        new_m = dot_nn(both, q[r, WIDE:2 * WIDE, :])
        res = new_k[0:MODES] - new_m[0:MODES] * theta2
        w2[r, 0:2 * MODES, :] = new
        w2[r, 2 * MODES:WIDE, :] = res
        ext[r + 1, R2LO:TOP, 0:lanes] = res
        q[r, 0:2 * MODES, :] = new_k
        q[r, WIDE:WIDE + 2 * MODES, :] = new_m
        q[r, 2 * WIDE:2 * WIDE + MODES, :] = new[0:MODES]
        return carry

    lax.fori_loop(0, rows, move_row, 0)
    exchange(2, R2LO, TOP)

    def last_row(r, total):
        _, k_out, m_out = operators(r, R2LO)
        q[r, 2 * MODES:WIDE, :] = k_out
        q[r, WIDE + 2 * MODES:2 * WIDE, :] = m_out
        return total + dot_nt(w2[r], q[r])

    table = lax.fori_loop(0, rows, last_row, jnp.zeros((WIDE, 128), F32))
    table = all_reduce(table, gr_x.at[1], gr_y.at[1], gr_xs.at[1], gr_xr.at[1], gr_ys.at[1], gr_yr.at[1])
    coef_t, search_t, ritz, _ = small_problem(table)
    both = jnp.concatenate([coef_t, search_t], axis=0) * math.sqrt(rows * lanes * ngx * ngy)
    for r in range(rows):
        new = dot_nn(both, w2[r])
        xo_ref[:, r, :] = new[0:MODES]
        po_ref[:, r, :] = new[MODES:2 * MODES]
    rz_ref[...] = jnp.sum(
        jnp.where(iota((MODES, 128), 0) == iota((MODES, 128), 1), ritz, 0.0), axis=0, keepdims=True)


def solution(mesh):
    ngx, ngy = mesh.shape["gx"], mesh.shape["gy"]

    def on_device(modes_start, search_start, stiffness, density):
        rows, lanes = stiffness.shape
        dma = pltpu.SemaphoreType.DMA
        modes, search, ritz = pl.pallas_call(
            functools.partial(kernel, ngx, ngy),
            out_shape=(
                jax.ShapeDtypeStruct(modes_start.shape, F32),
                jax.ShapeDtypeStruct(modes_start.shape, F32),
                jax.ShapeDtypeStruct((1, 128), F32),
            ),
            in_specs=[pl.BlockSpec(memory_space=pltpu.VMEM)] * 4,
            out_specs=[pl.BlockSpec(memory_space=pltpu.VMEM)] * 3,
            scratch_shapes=[
                pltpu.VMEM((rows + 2, TOP, lanes + 128), F32),
                pltpu.VMEM((rows, WIDE, lanes), F32),
                pltpu.VMEM((rows, 128, lanes), F32),
                pltpu.VMEM((rows, 8, lanes), F32),
                pltpu.VMEM((2, TOP, 128), F32),
                pltpu.VMEM((8, TOP, 128), F32),
                pltpu.VMEM((ngx, 2 * MODES, 128), F32),
                pltpu.VMEM((ngy, 2 * MODES, 128), F32),
                pltpu.VMEM((2, ngx, WIDE, 128), F32),
                pltpu.VMEM((2, ngy, WIDE, 128), F32),
                dma((3, 8)), dma((3, 8)),
                dma((ngx,)), dma((ngx,)), dma((ngy,)), dma((ngy,)),
                dma((2, ngx)), dma((2, ngx)), dma((2, ngy)), dma((2, ngy)),
            ],
            compiler_params=pltpu.CompilerParams(
                collective_id=0, has_side_effects=True, vmem_limit_bytes=40 * 1024 * 1024),
        )(modes_start, search_start, stiffness, density)
        return modes, search, ritz[0, 0:MODES]

    return jax.shard_map(
        on_device, mesh=mesh,
        in_specs=(P(None, "gx", "gy"), P(None, "gx", "gy"), P("gx", "gy"), P("gx", "gy")),
        out_specs=(P(None, "gx", "gy"), P(None, "gx", "gy"), P()),
        check_vma=False,
    )
```

```python
import functools
import math

import jax
import jax.numpy as jnp
from jax import lax
from jax.experimental import pallas as pl
from jax.experimental.pallas import tpu as pltpu
from jax.sharding import PartitionSpec as P

NZ = 16
MODES = 16
POWERS = (2, 2, 1, 1)
MESH = pl.DeviceIdType.MESH
F32 = jnp.float32
HIGHEST = lax.Precision.HIGHEST
WIDE = 3 * MODES
COEF, XLO, PLO, RLO, R2LO, TOP = 0, 8, 24, 40, 56, 72


def dot_nt(left, right):
    return lax.dot_general(left, right, (((1,), (1,)), ((), ())), precision=HIGHEST,
                           preferred_element_type=F32)


def dot_nn(left, right):
    return lax.dot_general(left, right, (((1,), (0,)), ((), ())), precision=HIGHEST,
                           preferred_element_type=F32)


def iota(shape, dim):
    return lax.broadcasted_iota(jnp.int32, shape, dim)


def jordan_pair(table, k):
    row_id = iota((table.shape[0], 1), 0)
    first, second = table[:, k:k + 1], table[:, k + 1:k + 2]
    top, low = table[k:k + 1, :], table[k + 1:k + 2, :]
    corner = top[:, k + 1:k + 2]
    inverse = 1.0 / top[:, k:k + 1]
    ratio = low[:, k:k + 1] * inverse
    low = (low - ratio * top) * (1.0 / (low[:, k + 1:k + 2] - ratio * corner))
    top = (top - corner * low) * inverse
    rest = table - first * top - second * low
    return jnp.where(row_id == k, top, jnp.where(row_id == k + 1, low, rest))


def orthonormal(gram, rows_t):
    count = gram.shape[0]
    row_id = iota((count, 1), 0)
    for k in range(0, count, 2):
        first, second = gram[:, k:k + 1], gram[:, k + 1:k + 2]
        corner = gram[k:k + 1, k + 1:k + 2]
        inverse = 1.0 / gram[k:k + 1, k:k + 1]
        ratio = gram[k + 1:k + 2, k:k + 1] * inverse
        factor = first * inverse
        other = (second - factor * corner) * (
            1.0 / (gram[k + 1:k + 2, k + 1:k + 2] - ratio * corner))
        factor = jnp.where(row_id > k, factor, 0.0)
        other = jnp.where(row_id > k + 1, other, 0.0)

        def eliminate(value):
            top = value[k:k + 1, :]
            return value - factor * top - other * (value[k + 1:k + 2, :] - ratio * top)

        gram, rows_t = eliminate(gram), eliminate(rows_t)
    diag = jnp.sum(jnp.where(iota(gram.shape, 0) == iota(gram.shape, 1), gram, 0.0),
                   axis=1, keepdims=True)
    return rows_t * lax.rsqrt(diag)


def small_problem(table):
    stiff = table[:, 0:WIDE]
    mass = table[:, WIDE:2 * WIDE]
    cross = table[:, 2 * WIDE:2 * WIDE + MODES]
    solved = table
    corner = jnp.concatenate(
        [cross[0:MODES], (iota((MODES, MODES), 0) == iota((MODES, MODES), 1)).astype(F32)], axis=1)
    for k in range(0, WIDE, 2):
        solved = jordan_pair(solved, k)
        if k < MODES:
            corner = jordan_pair(corner, k)
    step = solved[:, WIDE:2 * WIDE]
    coef_t = (iota((MODES, WIDE), 0) == iota((MODES, WIDE), 1)).astype(F32)
    for power in POWERS:
        for _ in range(power):
            coef_t = dot_nt(coef_t, step)
        coef_t = orthonormal(dot_nt(dot_nn(coef_t, mass), coef_t), coef_t)
    ritz = jnp.sum(dot_nn(coef_t, stiff) * coef_t, axis=1, keepdims=True)
    norm = jnp.sum(dot_nn(coef_t, mass) * coef_t, axis=1, keepdims=True)
    rest_t = jnp.where(iota((MODES, WIDE), 1) >= MODES, coef_t, 0.0)
    top = dot_nn(dot_nn(rest_t, cross), corner[:, MODES:2 * MODES])
    search_t = rest_t - jnp.concatenate([top, jnp.zeros((MODES, WIDE - MODES), F32)], axis=1)
    return coef_t, search_t, ritz, ritz / norm


def kernel(ngx, ngy, x_hbm, p_hbm, s_hbm, d_hbm, xo_ref, po_ref, rz_ref,
           x_ref, p_ref, s_ref, d_ref, ext, w2, q, kx, k0, pk, side, th_x, th_y, sc_src, sc_dst, gr_y, gat,
           in_sem, h_send, h_recv, th_xs, th_xr, th_ys, th_yr,
           rs_s, rs_r, gr_ys, gr_yr, ag_s, ag_r):
    rows, lanes = s_ref.shape
    full = lanes + 128
    gx, gy = lax.axis_index("gx"), lax.axis_index("gy")
    lane_id = iota((1, full), 1)
    depth = lane_id % NZ
    low = (depth >= 1).astype(F32)
    high = (depth <= NZ - 2).astype(F32)
    tile_id = iota((1, 128), 1)
    inputs = [pltpu.make_async_copy(src, dst, in_sem.at[i]) for i, (src, dst) in enumerate(
        ((s_hbm, s_ref), (d_hbm, d_ref), (x_hbm, x_ref), (p_hbm, p_ref)))]
    for copy in inputs:
        copy.start()

    barrier = pltpu.get_barrier_semaphore()
    for o in range(1, ngx):
        pl.semaphore_signal(barrier, inc=1, device_id=(lax.rem(gx + o, ngx), gy), device_id_type=MESH)
    for o in range(1, ngy):
        pl.semaphore_signal(barrier, inc=1, device_id=(gx, lax.rem(gy + o, ngy)), device_id_type=MESH)

    def exists(dx, dy):
        good = None
        for cond in ([gx > 0] if dx < 0 else [gx < ngx - 1] if dx > 0 else []) + (
                [gy > 0] if dy < 0 else [gy < ngy - 1] if dy > 0 else []):
            good = cond if good is None else jnp.logical_and(good, cond)
        return good

    for dx in (1, ngx - 1):
        for dy in (1, ngy - 1):
            pl.semaphore_signal(barrier, inc=1, device_id_type=MESH,
                                device_id=(lax.rem(gx + dx, ngx), lax.rem(gy + dy, ngy)))
    pl.semaphore_wait(barrier, ngx - 1 + ngy - 1 + 4)

    for copy in inputs:
        copy.wait()
    q_pad = q.shape[1] - 2 * WIDE - MODES
    for r in range(rows):
        modes_row = x_ref[:, r, :]
        ext[r + 1, XLO:PLO, 0:lanes] = modes_row
        ext[r + 1, PLO:RLO, 0:lanes] = p_ref[:, r, :]
        ext[r + 1, COEF:COEF + 8, 0:lanes] = jnp.concatenate(
            [s_ref[r:r + 1, :], jnp.sqrt(d_ref[r:r + 1, :]), jnp.zeros((6, lanes), F32)], axis=0)
        q[r, 2 * WIDE:2 * WIDE + MODES, :] = modes_row
        q[r, 2 * WIDE + MODES:, :] = jnp.zeros((q_pad, lanes), F32)

    steps = [(dx, dy) for dx in (-1, 0, 1) for dy in (-1, 0, 1) if (dx, dy) != (0, 0)]

    def send_rims(phase, lo, hi):
        left = jnp.zeros((hi - lo, 128), F32)
        right = jnp.zeros((hi - lo, 128), F32)
        for r in range(rows):
            here = jnp.logical_and(tile_id >= NZ * r, tile_id < NZ * (r + 1))
            first = ext[r + 1, lo:hi, 0:128]
            last = pltpu.roll(ext[r + 1, lo:hi, lanes - 128:lanes], NZ, 1)
            if r:
                first, last = pltpu.roll(first, NZ * r, 1), pltpu.roll(last, NZ * r, 1)
            left, right = jnp.where(here, first, left), jnp.where(here, last, right)
        pk[0, lo:hi, :] = left
        pk[1, lo:hi, :] = right
        copies = []
        for i, (dx, dy) in enumerate(steps):
            back = steps.index((-dx, -dy))
            if dy == 0:
                src = ext.at[1 if dx < 0 else rows, lo:hi, 0:lanes]
                dst = ext.at[rows + 1 if dx < 0 else 0, lo:hi, 0:lanes]
            else:
                src = pk.at[0 if dy < 0 else 1, lo:hi]
                dst = side.at[back, lo:hi]
            copy = pltpu.make_async_remote_copy(
                src_ref=src, dst_ref=dst, send_sem=h_send.at[phase, i], recv_sem=h_recv.at[phase, back],
                device_id=(gx + dx, gy + dy), device_id_type=MESH)
            copies.append(copy)
            there = exists(dx, dy)

            @pl.when(there)
            def _(copy=copy):
                copy.start()

            @pl.when(jnp.logical_not(there))
            def _(i=i, dx=dx, dy=dy):
                if dy == 0:
                    ext[0 if dx < 0 else rows + 1, lo:hi, 0:lanes] = jnp.zeros((hi - lo, lanes), F32)
                else:
                    side[i, lo:hi, :] = jnp.zeros((hi - lo, 128), F32)
        return copies

    def take_rims(copies, lo, hi):
        for i, (dx, dy) in enumerate(steps):
            back = steps.index((-dx, -dy))

            @pl.when(exists(dx, dy))
            def _(i=i, back=back):
                copies[i].wait_send()
                copies[back].wait_recv()
        for e in range(rows + 2):
            dx, r = (-1, rows - 1) if e == 0 else (1, 0) if e == rows + 1 else (0, e - 1)
            from_left = side[steps.index((dx, -1)), lo:hi, :]
            from_right = side[steps.index((dx, 1)), lo:hi, :]
            from_left = pltpu.roll(from_left, (112 - NZ * r) % 128, 1) if (112 - NZ * r) % 128 else from_left
            from_right = pltpu.roll(from_right, (128 - NZ * r) % 128, 1) if r else from_right
            ext[e, lo:hi, lanes:full] = jnp.where(
                tile_id < NZ, from_right, jnp.where(tile_id >= 128 - NZ, from_left, 0.0))

    def swap_line(size, me, place, source, slots, send, recv):
        copies = []
        for o in range(1, size):
            to = lax.rem(me + o, size)
            copy = pltpu.make_async_remote_copy(
                src_ref=source(to), dst_ref=slots.at[me], send_sem=send.at[o], recv_sem=recv.at[o],
                device_id=place(to), device_id_type=MESH)
            copy.start()
            copies.append(copy)
        for copy in copies:
            copy.wait()

    def add_up(slots, size):
        parts = [slots[o] for o in range(size)]
        while len(parts) > 1:
            parts = [a + b for a, b in zip(parts[::2], parts[1::2])] + parts[len(parts) // 2 * 2:]
        return parts[0]

    def in_column(other):
        return other, gy

    def in_row(other):
        return gx, other

    def line_sum(size, me, place, value, slots, send, recv):
        slots[me] = value
        swap_line(size, me, place, lambda to: slots.at[me], slots, send, recv)
        return add_up(slots, size)

    def table_sum(it, table):
        block = -(-WIDE // ngx)
        tall = sc_src.shape[2]
        for o in range(ngx):
            piece = table[min(WIDE, block * o):min(WIDE, block * (o + 1))]
            short = tall - piece.shape[0]
            if short == tall:
                piece = jnp.zeros((tall, 128), F32)
            elif short:
                piece = jnp.concatenate([piece, jnp.zeros((short, 128), F32)], axis=0)
            sc_src[it, o] = piece
        sc_dst[it, gx] = sc_src[it, gx]
        swap_line(ngx, gx, in_column, lambda to: sc_src.at[it, to], sc_dst.at[it], rs_s.at[it], rs_r.at[it])
        part = add_up(sc_dst.at[it], ngx)
        part = line_sum(ngy, gy, in_row, part, gr_y.at[it], gr_ys.at[it], gr_yr.at[it])
        gat[it, gx] = part
        swap_line(ngx, gx, in_column, lambda to: gat.at[it, gx], gat.at[it], ag_s.at[it], ag_r.at[it])
        return jnp.concatenate([gat[it, o, 0:block] for o in range(-(-WIDE // block))], axis=0)[0:WIDE]

    def plane(value, center, edge):
        if center == 1.0:
            value = value + edge * (pltpu.roll(value, 1, 1) * low + pltpu.roll(value, full - 1, 1) * high)
            return value + edge * (pltpu.roll(value, NZ, 1) + pltpu.roll(value, full - NZ, 1))
        value = center * value + (pltpu.roll(value, 1, 1) * low + pltpu.roll(value, full - 1, 1) * high)
        return center * value + (pltpu.roll(value, NZ, 1) + pltpu.roll(value, full - NZ, 1))

    def operators(r, lo):
        before, here, after = [ext[r + j, lo:lo + MODES, :] for j in range(3)]
        s_b, s_h, s_a = [ext[r + j, 0:1, :] for j in range(3)]
        d_b, d_h, d_a = [ext[r + j, 1:2, :] for j in range(3)]
        plain = plane(here + 0.5 * (before + after), 1.0, 0.5)
        stiff = plane(s_h * here + 0.5 * (s_b * before + s_a * after), 1.0, 0.5)
        mass = plane(4.0 * (d_h * here) + (d_b * before + d_a * after), 4.0, 1.0)
        field = here[:, 0:lanes]
        k_out = field * k0[r, 0:1, :] - s_h[:, 0:lanes] * plain[:, 0:lanes] - stiff[:, 0:lanes]
        m_out = (d_h[:, 0:lanes] * (1.0 / 216.0)) * mass[:, 0:lanes]
        return field, k_out, m_out

    rims = send_rims(0, COEF, PLO)
    search_rims = send_rims(1, PLO, RLO)
    take_rims(rims, COEF, PLO)

    def coef_row(r, carry):
        before, here, after = [ext[r + j, 0:8, :] for j in range(3)]
        near = plane(here + 0.5 * (before + after), 1.0, 0.5)
        k0[r] = 8.0 * here[:, 0:lanes] + near[:, 0:lanes]
        return carry

    lax.fori_loop(0, rows, coef_row, 0)

    def fold(value):
        total = value[:, 0:128]
        for j in range(1, lanes // 128):
            total = total + value[:, 128 * j:128 * (j + 1)]
        return total

    def mode_row(r, carry):
        field, k_out, m_out = operators(r, XLO)
        q[r, 0:MODES, :] = k_out
        q[r, WIDE:WIDE + MODES, :] = m_out
        return carry[0] + fold(field * k_out), carry[1] + fold(field * m_out)

    zero = jnp.zeros((MODES, 128), F32)
    numer, denom = lax.fori_loop(0, rows, mode_row, (zero, zero))
    pair = iota((2 * MODES, 128), 0) == iota((2 * MODES, 128), 1)
    sums = jnp.sum(jnp.concatenate([numer, denom], axis=0), axis=1, keepdims=True)
    sums = jnp.broadcast_to(jnp.sum(jnp.where(pair, sums, 0.0), axis=0, keepdims=True), (8, 128))
    sums = line_sum(ngx, gx, in_column, sums, th_x, th_xs, th_xr)
    sums = line_sum(ngy, gy, in_row, sums, th_y, th_ys, th_yr)
    sums = jnp.sum(jnp.where(pair, sums[0:1], 0.0), axis=1, keepdims=True)
    theta = sums[0:MODES] / sums[MODES:2 * MODES]

    def residual_row(r, carry):
        ext[r + 1, RLO:R2LO, 0:lanes] = q[r, 0:MODES, :] - q[r, WIDE:WIDE + MODES, :] * theta
        return carry

    lax.fori_loop(0, rows, residual_row, 0)
    rims = send_rims(2, RLO, R2LO)
    take_rims(search_rims, PLO, RLO)

    def search_row(r, carry):
        _, k_out, m_out = operators(r, PLO)
        q[r, MODES:2 * MODES, :] = k_out
        q[r, WIDE + MODES:WIDE + 2 * MODES, :] = m_out
        return carry

    lax.fori_loop(0, rows, search_row, 0)
    take_rims(rims, RLO, R2LO)

    def rest_row(r, total):
        _, k_out, m_out = operators(r, RLO)
        q[r, 2 * MODES:WIDE, :] = k_out
        q[r, WIDE + 2 * MODES:2 * WIDE, :] = m_out
        return total + dot_nt(ext[r + 1, XLO:R2LO, 0:lanes], q[r])

    table = table_sum(0, lax.fori_loop(0, rows, rest_row, jnp.zeros((WIDE, 128), F32)))
    coef_t, search_t, _, theta2 = small_problem(table)
    both = jnp.concatenate([coef_t, search_t], axis=0)

    def next_residual_row(r, carry):
        new_k = dot_nn(coef_t, q[r, 0:WIDE, :])
        new_m = dot_nn(coef_t, q[r, WIDE:2 * WIDE, :])
        res = new_k - new_m * theta2
        kx[r, 0:MODES, :] = new_k
        kx[r, MODES:2 * MODES, :] = new_m
        w2[r, 2 * MODES:WIDE, :] = res
        ext[r + 1, R2LO:TOP, 0:lanes] = res
        return carry

    lax.fori_loop(0, rows, next_residual_row, 0)
    rims = send_rims(3, R2LO, TOP)

    def move_row(r, carry):
        new = dot_nn(both, ext[r + 1, XLO:R2LO, 0:lanes])
        new_k = dot_nn(search_t, q[r, 0:WIDE, :])
        new_m = dot_nn(search_t, q[r, WIDE:2 * WIDE, :])
        w2[r, 0:2 * MODES, :] = new
        q[r, 0:MODES, :] = kx[r, 0:MODES, :]
        q[r, MODES:2 * MODES, :] = new_k
        q[r, WIDE:WIDE + MODES, :] = kx[r, MODES:2 * MODES, :]
        q[r, WIDE + MODES:WIDE + 2 * MODES, :] = new_m
        q[r, 2 * WIDE:2 * WIDE + MODES, :] = new[0:MODES]
        return carry

    lax.fori_loop(0, rows, move_row, 0)
    take_rims(rims, R2LO, TOP)

    def last_row(r, total):
        _, k_out, m_out = operators(r, R2LO)
        q[r, 2 * MODES:WIDE, :] = k_out
        q[r, WIDE + 2 * MODES:2 * WIDE, :] = m_out
        return total + dot_nt(w2[r], q[r])

    table = table_sum(1, lax.fori_loop(0, rows, last_row, jnp.zeros((WIDE, 128), F32)))
    coef_t, search_t, ritz, _ = small_problem(table)
    both = jnp.concatenate([coef_t, search_t], axis=0) * math.sqrt(rows * lanes * ngx * ngy)
    for r in range(rows):
        new = dot_nn(both, w2[r])
        xo_ref[:, r, :] = new[0:MODES]
        po_ref[:, r, :] = new[MODES:2 * MODES]
    rz_ref[...] = jnp.sum(
        jnp.where(iota((MODES, 128), 0) == iota((MODES, 128), 1), ritz, 0.0), axis=0, keepdims=True)


def solution(mesh):
    ngx, ngy = mesh.shape["gx"], mesh.shape["gy"]

    def on_device(modes_start, search_start, stiffness, density):
        rows, lanes = stiffness.shape
        dma = pltpu.SemaphoreType.DMA
        tall = -(-(-(-WIDE // ngx)) // 8) * 8
        modes, search, ritz = pl.pallas_call(
            functools.partial(kernel, ngx, ngy),
            out_shape=(
                jax.ShapeDtypeStruct(modes_start.shape, F32),
                jax.ShapeDtypeStruct(modes_start.shape, F32),
                jax.ShapeDtypeStruct((1, 128), F32),
            ),
            in_specs=[pl.BlockSpec(memory_space=pl.ANY)] * 4,
            out_specs=[pl.BlockSpec(memory_space=pltpu.VMEM)] * 3,
            scratch_shapes=[
                pltpu.VMEM(modes_start.shape, F32),
                pltpu.VMEM(modes_start.shape, F32),
                pltpu.VMEM((rows, lanes), F32),
                pltpu.VMEM((rows, lanes), F32),
                pltpu.VMEM((rows + 2, TOP, lanes + 128), F32),
                pltpu.VMEM((rows, WIDE, lanes), F32),
                pltpu.VMEM((rows, 128, lanes), F32),
                pltpu.VMEM((rows, 2 * MODES, lanes), F32),
                pltpu.VMEM((rows, 8, lanes), F32),
                pltpu.VMEM((2, TOP, 128), F32),
                pltpu.VMEM((8, TOP, 128), F32),
                pltpu.VMEM((ngx, 8, 128), F32),
                pltpu.VMEM((ngy, 8, 128), F32),
                pltpu.VMEM((2, ngx, tall, 128), F32),
                pltpu.VMEM((2, ngx, tall, 128), F32),
                pltpu.VMEM((2, ngy, tall, 128), F32),
                pltpu.VMEM((2, ngx, tall, 128), F32),
                dma((4,)), dma((4, 8)), dma((4, 8)),
                dma((ngx,)), dma((ngx,)), dma((ngy,)), dma((ngy,)),
                dma((2, ngx)), dma((2, ngx)), dma((2, ngy)), dma((2, ngy)), dma((2, ngx)), dma((2, ngx)),
            ],
            compiler_params=pltpu.CompilerParams(
                collective_id=0, has_side_effects=True, vmem_limit_bytes=40 * 1024 * 1024),
        )(modes_start, search_start, stiffness, density)
        return modes, search, ritz[0, 0:MODES]

    return jax.shard_map(
        on_device, mesh=mesh,
        in_specs=(P(None, "gx", "gy"), P(None, "gx", "gy"), P("gx", "gy"), P("gx", "gy")),
        out_specs=(P(None, "gx", "gy"), P(None, "gx", "gy"), P()),
        check_vma=False,
    )
```

```python
import functools
import math

import jax
import jax.numpy as jnp
from jax import lax
from jax.experimental import pallas as pl
from jax.experimental.pallas import tpu as pltpu
from jax.sharding import PartitionSpec as P

NZ = 16
MODES = 16
POWERS = (2, 2, 1, 1)
MESH = pl.DeviceIdType.MESH
F32 = jnp.float32
HIGHEST = lax.Precision.HIGHEST
WIDE = 3 * MODES
COEF, XLO, PLO, RLO, R2LO, TOP = 0, 8, 24, 40, 56, 72


def dot_nt(left, right):
    return lax.dot_general(left, right, (((1,), (1,)), ((), ())), precision=HIGHEST,
                           preferred_element_type=F32)


def dot_nn(left, right):
    return lax.dot_general(left, right, (((1,), (0,)), ((), ())), precision=HIGHEST,
                           preferred_element_type=F32)


def iota(shape, dim):
    return lax.broadcasted_iota(jnp.int32, shape, dim)


def jordan_step(table, k):
    rows = table.shape[0]
    pivot_row = table[k:k + 1, :] * (1.0 / table[k:k + 1, k:k + 1])
    return jnp.where(iota((rows, 1), 0) == k, pivot_row, table - table[:, k:k + 1] * pivot_row)


def orthonormal(gram, rows_t):
    count = gram.shape[0]
    row_id = iota((count, 1), 0)
    for k in range(count - 1):
        factor = jnp.where(row_id > k, gram[:, k:k + 1] * (1.0 / gram[k:k + 1, k:k + 1]), 0.0)
        gram, rows_t = gram - factor * gram[k:k + 1, :], rows_t - factor * rows_t[k:k + 1, :]
    diag = jnp.sum(jnp.where(iota(gram.shape, 0) == iota(gram.shape, 1), gram, 0.0),
                   axis=1, keepdims=True)
    return rows_t * lax.rsqrt(diag)


def small_problem(table):
    stiff = table[:, 0:WIDE]
    mass = table[:, WIDE:2 * WIDE]
    cross = table[:, 2 * WIDE:2 * WIDE + MODES]
    solved = table
    corner = jnp.concatenate(
        [cross[0:MODES], (iota((MODES, MODES), 0) == iota((MODES, MODES), 1)).astype(F32)], axis=1)
    for k in range(WIDE):
        solved = jordan_step(solved, k)
        if k < MODES:
            corner = jordan_step(corner, k)
    step = solved[:, WIDE:2 * WIDE]
    coef_t = (iota((MODES, WIDE), 0) == iota((MODES, WIDE), 1)).astype(F32)
    for power in POWERS:
        for _ in range(power):
            coef_t = dot_nt(coef_t, step)
        coef_t = orthonormal(dot_nt(dot_nn(coef_t, mass), coef_t), coef_t)
    ritz = jnp.sum(dot_nn(coef_t, stiff) * coef_t, axis=1, keepdims=True)
    norm = jnp.sum(dot_nn(coef_t, mass) * coef_t, axis=1, keepdims=True)
    rest_t = jnp.where(iota((MODES, WIDE), 1) >= MODES, coef_t, 0.0)
    top = dot_nn(dot_nn(rest_t, cross), corner[:, MODES:2 * MODES])
    search_t = rest_t - jnp.concatenate([top, jnp.zeros((MODES, WIDE - MODES), F32)], axis=1)
    return coef_t, search_t, ritz, ritz / norm


def kernel(ngx, ngy, x_hbm, p_hbm, s_hbm, d_hbm, xo_ref, po_ref, rz_ref,
           x_ref, p_ref, s_ref, d_ref, ext, w2, q, kx, k0, pk, side, th_x, th_y, gr_x, gr_y,
           in_sem, h_send, h_recv, th_xs, th_xr, th_ys, th_yr,
           gr_xs, gr_xr, gr_ys, gr_yr):
    rows, lanes = s_ref.shape
    full = lanes + 128
    gx, gy = lax.axis_index("gx"), lax.axis_index("gy")
    lane_id = iota((1, full), 1)
    depth = lane_id % NZ
    low = (depth >= 1).astype(F32)
    high = (depth <= NZ - 2).astype(F32)
    tile_id = iota((1, 128), 1)
    inputs = [pltpu.make_async_copy(src, dst, in_sem.at[i]) for i, (src, dst) in enumerate(
        ((s_hbm, s_ref), (d_hbm, d_ref), (x_hbm, x_ref), (p_hbm, p_ref)))]
    for copy in inputs:
        copy.start()

    barrier = pltpu.get_barrier_semaphore()
    for o in range(1, ngx):
        pl.semaphore_signal(barrier, inc=1, device_id=(lax.rem(gx + o, ngx), gy), device_id_type=MESH)
    for o in range(1, ngy):
        pl.semaphore_signal(barrier, inc=1, device_id=(gx, lax.rem(gy + o, ngy)), device_id_type=MESH)

    def exists(dx, dy):
        good = None
        for cond in ([gx > 0] if dx < 0 else [gx < ngx - 1] if dx > 0 else []) + (
                [gy > 0] if dy < 0 else [gy < ngy - 1] if dy > 0 else []):
            good = cond if good is None else jnp.logical_and(good, cond)
        return good

    for dx in (1, ngx - 1):
        for dy in (1, ngy - 1):
            pl.semaphore_signal(barrier, inc=1, device_id_type=MESH,
                                device_id=(lax.rem(gx + dx, ngx), lax.rem(gy + dy, ngy)))
    pl.semaphore_wait(barrier, ngx - 1 + ngy - 1 + 4)

    for copy in inputs:
        copy.wait()
    q_pad = q.shape[1] - 2 * WIDE - MODES
    for r in range(rows):
        modes_row = x_ref[:, r, :]
        ext[r + 1, XLO:PLO, 0:lanes] = modes_row
        ext[r + 1, PLO:RLO, 0:lanes] = p_ref[:, r, :]
        ext[r + 1, COEF:COEF + 8, 0:lanes] = jnp.concatenate(
            [s_ref[r:r + 1, :], jnp.sqrt(d_ref[r:r + 1, :]), jnp.zeros((6, lanes), F32)], axis=0)
        q[r, 2 * WIDE:2 * WIDE + MODES, :] = modes_row
        q[r, 2 * WIDE + MODES:, :] = jnp.zeros((q_pad, lanes), F32)

    steps = [(dx, dy) for dx in (-1, 0, 1) for dy in (-1, 0, 1) if (dx, dy) != (0, 0)]

    def send_rims(phase, lo, hi):
        left = jnp.zeros((hi - lo, 128), F32)
        right = jnp.zeros((hi - lo, 128), F32)
        for r in range(rows):
            here = jnp.logical_and(tile_id >= NZ * r, tile_id < NZ * (r + 1))
            first = ext[r + 1, lo:hi, 0:128]
            last = pltpu.roll(ext[r + 1, lo:hi, lanes - 128:lanes], NZ, 1)
            if r:
                first, last = pltpu.roll(first, NZ * r, 1), pltpu.roll(last, NZ * r, 1)
            left, right = jnp.where(here, first, left), jnp.where(here, last, right)
        pk[0, lo:hi, :] = left
        pk[1, lo:hi, :] = right
        copies = []
        for i, (dx, dy) in enumerate(steps):
            back = steps.index((-dx, -dy))
            if dy == 0:
                src = ext.at[1 if dx < 0 else rows, lo:hi, 0:lanes]
                dst = ext.at[rows + 1 if dx < 0 else 0, lo:hi, 0:lanes]
            else:
                src = pk.at[0 if dy < 0 else 1, lo:hi]
                dst = side.at[back, lo:hi]
            copy = pltpu.make_async_remote_copy(
                src_ref=src, dst_ref=dst, send_sem=h_send.at[phase, i], recv_sem=h_recv.at[phase, back],
                device_id=(gx + dx, gy + dy), device_id_type=MESH)
            copies.append(copy)
            there = exists(dx, dy)

            @pl.when(there)
            def _(copy=copy):
                copy.start()

            @pl.when(jnp.logical_not(there))
            def _(i=i, dx=dx, dy=dy):
                if dy == 0:
                    ext[0 if dx < 0 else rows + 1, lo:hi, 0:lanes] = jnp.zeros((hi - lo, lanes), F32)
                else:
                    side[i, lo:hi, :] = jnp.zeros((hi - lo, 128), F32)
        return copies

    def take_rims(copies, lo, hi):
        for i, (dx, dy) in enumerate(steps):
            back = steps.index((-dx, -dy))

            @pl.when(exists(dx, dy))
            def _(i=i, back=back):
                copies[i].wait_send()
                copies[back].wait_recv()
        for e in range(rows + 2):
            dx, r = (-1, rows - 1) if e == 0 else (1, 0) if e == rows + 1 else (0, e - 1)
            from_left = side[steps.index((dx, -1)), lo:hi, :]
            from_right = side[steps.index((dx, 1)), lo:hi, :]
            from_left = pltpu.roll(from_left, (112 - NZ * r) % 128, 1) if (112 - NZ * r) % 128 else from_left
            from_right = pltpu.roll(from_right, (128 - NZ * r) % 128, 1) if r else from_right
            ext[e, lo:hi, lanes:full] = jnp.where(
                tile_id < NZ, from_right, jnp.where(tile_id >= 128 - NZ, from_left, 0.0))

    def swap_line(size, me, place, source, slots, send, recv):
        copies = []
        for o in range(1, size):
            to = lax.rem(me + o, size)
            copy = pltpu.make_async_remote_copy(
                src_ref=source(to), dst_ref=slots.at[me], send_sem=send.at[o], recv_sem=recv.at[o],
                device_id=place(to), device_id_type=MESH)
            copy.start()
            copies.append(copy)
        for copy in copies:
            copy.wait()

    def add_up(slots, size):
        parts = [slots[o] for o in range(size)]
        while len(parts) > 1:
            parts = [a + b for a, b in zip(parts[::2], parts[1::2])] + parts[len(parts) // 2 * 2:]
        return parts[0]

    def in_column(other):
        return other, gy

    def in_row(other):
        return gx, other

    def line_sum(size, me, place, value, slots, send, recv):
        slots[me] = value
        swap_line(size, me, place, lambda to: slots.at[me], slots, send, recv)
        return add_up(slots, size)

    def table_sum(it, table):
        table = line_sum(ngx, gx, in_column, table, gr_x.at[it], gr_xs.at[it], gr_xr.at[it])
        return line_sum(ngy, gy, in_row, table, gr_y.at[it], gr_ys.at[it], gr_yr.at[it])

    def plane(value, center, edge):
        if center == 1.0:
            value = value + edge * (pltpu.roll(value, 1, 1) * low + pltpu.roll(value, full - 1, 1) * high)
            return value + edge * (pltpu.roll(value, NZ, 1) + pltpu.roll(value, full - NZ, 1))
        value = center * value + (pltpu.roll(value, 1, 1) * low + pltpu.roll(value, full - 1, 1) * high)
        return center * value + (pltpu.roll(value, NZ, 1) + pltpu.roll(value, full - NZ, 1))

    def operators(r, lo):
        before, here, after = [ext[r + j, lo:lo + MODES, :] for j in range(3)]
        s_b, s_h, s_a = [ext[r + j, 0:1, :] for j in range(3)]
        d_b, d_h, d_a = [ext[r + j, 1:2, :] for j in range(3)]
        plain = plane(here + 0.5 * (before + after), 1.0, 0.5)
        stiff = plane(s_h * here + 0.5 * (s_b * before + s_a * after), 1.0, 0.5)
        mass = plane(4.0 * (d_h * here) + (d_b * before + d_a * after), 4.0, 1.0)
        field = here[:, 0:lanes]
        k_out = field * k0[r, 0:1, :] - s_h[:, 0:lanes] * plain[:, 0:lanes] - stiff[:, 0:lanes]
        m_out = (d_h[:, 0:lanes] * (1.0 / 216.0)) * mass[:, 0:lanes]
        return field, k_out, m_out

    rims = send_rims(0, COEF, PLO)
    search_rims = send_rims(1, PLO, RLO)
    take_rims(rims, COEF, PLO)

    def coef_row(r, carry):
        before, here, after = [ext[r + j, 0:8, :] for j in range(3)]
        near = plane(here + 0.5 * (before + after), 1.0, 0.5)
        k0[r] = 8.0 * here[:, 0:lanes] + near[:, 0:lanes]
        return carry

    lax.fori_loop(0, rows, coef_row, 0)

    def fold(value):
        total = value[:, 0:128]
        for j in range(1, lanes // 128):
            total = total + value[:, 128 * j:128 * (j + 1)]
        return total

    def mode_row(r, carry):
        field, k_out, m_out = operators(r, XLO)
        q[r, 0:MODES, :] = k_out
        q[r, WIDE:WIDE + MODES, :] = m_out
        return carry[0] + fold(field * k_out), carry[1] + fold(field * m_out)

    zero = jnp.zeros((MODES, 128), F32)
    numer, denom = lax.fori_loop(0, rows, mode_row, (zero, zero))
    pair = iota((2 * MODES, 128), 0) == iota((2 * MODES, 128), 1)
    sums = jnp.sum(jnp.concatenate([numer, denom], axis=0), axis=1, keepdims=True)
    sums = jnp.broadcast_to(jnp.sum(jnp.where(pair, sums, 0.0), axis=0, keepdims=True), (8, 128))
    sums = line_sum(ngx, gx, in_column, sums, th_x, th_xs, th_xr)
    sums = line_sum(ngy, gy, in_row, sums, th_y, th_ys, th_yr)
    sums = jnp.sum(jnp.where(pair, sums[0:1], 0.0), axis=1, keepdims=True)
    theta = sums[0:MODES] / sums[MODES:2 * MODES]

    def residual_row(r, carry):
        ext[r + 1, RLO:R2LO, 0:lanes] = q[r, 0:MODES, :] - q[r, WIDE:WIDE + MODES, :] * theta
        return carry

    lax.fori_loop(0, rows, residual_row, 0)
    rims = send_rims(2, RLO, R2LO)
    take_rims(search_rims, PLO, RLO)

    def search_row(r, carry):
        _, k_out, m_out = operators(r, PLO)
        q[r, MODES:2 * MODES, :] = k_out
        q[r, WIDE + MODES:WIDE + 2 * MODES, :] = m_out
        return carry

    lax.fori_loop(0, rows, search_row, 0)
    take_rims(rims, RLO, R2LO)

    def rest_row(r, total):
        _, k_out, m_out = operators(r, RLO)
        q[r, 2 * MODES:WIDE, :] = k_out
        q[r, WIDE + 2 * MODES:2 * WIDE, :] = m_out
        return total + dot_nt(ext[r + 1, XLO:R2LO, 0:lanes], q[r])

    table = table_sum(0, lax.fori_loop(0, rows, rest_row, jnp.zeros((WIDE, 128), F32)))
    coef_t, search_t, _, theta2 = small_problem(table)
    both = jnp.concatenate([coef_t, search_t], axis=0)

    def next_residual_row(r, carry):
        new_k = dot_nn(coef_t, q[r, 0:WIDE, :])
        new_m = dot_nn(coef_t, q[r, WIDE:2 * WIDE, :])
        res = new_k - new_m * theta2
        kx[r, 0:MODES, :] = new_k
        kx[r, MODES:2 * MODES, :] = new_m
        w2[r, 2 * MODES:WIDE, :] = res
        ext[r + 1, R2LO:TOP, 0:lanes] = res
        return carry

    lax.fori_loop(0, rows, next_residual_row, 0)
    rims = send_rims(3, R2LO, TOP)

    def move_row(r, carry):
        new = dot_nn(both, ext[r + 1, XLO:R2LO, 0:lanes])
        new_k = dot_nn(search_t, q[r, 0:WIDE, :])
        new_m = dot_nn(search_t, q[r, WIDE:2 * WIDE, :])
        w2[r, 0:2 * MODES, :] = new
        q[r, 0:MODES, :] = kx[r, 0:MODES, :]
        q[r, MODES:2 * MODES, :] = new_k
        q[r, WIDE:WIDE + MODES, :] = kx[r, MODES:2 * MODES, :]
        q[r, WIDE + MODES:WIDE + 2 * MODES, :] = new_m
        q[r, 2 * WIDE:2 * WIDE + MODES, :] = new[0:MODES]
        return carry

    lax.fori_loop(0, rows, move_row, 0)
    take_rims(rims, R2LO, TOP)

    def last_row(r, total):
        _, k_out, m_out = operators(r, R2LO)
        q[r, 2 * MODES:WIDE, :] = k_out
        q[r, WIDE + 2 * MODES:2 * WIDE, :] = m_out
        return total + dot_nt(w2[r], q[r])

    table = table_sum(1, lax.fori_loop(0, rows, last_row, jnp.zeros((WIDE, 128), F32)))
    coef_t, search_t, ritz, _ = small_problem(table)
    both = jnp.concatenate([coef_t, search_t], axis=0) * math.sqrt(rows * lanes * ngx * ngy)
    for r in range(rows):
        new = dot_nn(both, w2[r])
        xo_ref[:, r, :] = new[0:MODES]
        po_ref[:, r, :] = new[MODES:2 * MODES]
    rz_ref[...] = jnp.sum(
        jnp.where(iota((MODES, 128), 0) == iota((MODES, 128), 1), ritz, 0.0), axis=0, keepdims=True)


def solution(mesh):
    ngx, ngy = mesh.shape["gx"], mesh.shape["gy"]

    def on_device(modes_start, search_start, stiffness, density):
        rows, lanes = stiffness.shape
        dma = pltpu.SemaphoreType.DMA
        modes, search, ritz = pl.pallas_call(
            functools.partial(kernel, ngx, ngy),
            out_shape=(
                jax.ShapeDtypeStruct(modes_start.shape, F32),
                jax.ShapeDtypeStruct(modes_start.shape, F32),
                jax.ShapeDtypeStruct((1, 128), F32),
            ),
            in_specs=[pl.BlockSpec(memory_space=pl.ANY)] * 4,
            out_specs=[pl.BlockSpec(memory_space=pltpu.VMEM)] * 3,
            scratch_shapes=[
                pltpu.VMEM(modes_start.shape, F32),
                pltpu.VMEM(modes_start.shape, F32),
                pltpu.VMEM((rows, lanes), F32),
                pltpu.VMEM((rows, lanes), F32),
                pltpu.VMEM((rows + 2, TOP, lanes + 128), F32),
                pltpu.VMEM((rows, WIDE, lanes), F32),
                pltpu.VMEM((rows, 128, lanes), F32),
                pltpu.VMEM((rows, 2 * MODES, lanes), F32),
                pltpu.VMEM((rows, 8, lanes), F32),
                pltpu.VMEM((2, TOP, 128), F32),
                pltpu.VMEM((8, TOP, 128), F32),
                pltpu.VMEM((ngx, 8, 128), F32),
                pltpu.VMEM((ngy, 8, 128), F32),
                pltpu.VMEM((2, ngx, WIDE, 128), F32),
                pltpu.VMEM((2, ngy, WIDE, 128), F32),
                dma((4,)), dma((4, 8)), dma((4, 8)),
                dma((ngx,)), dma((ngx,)), dma((ngy,)), dma((ngy,)),
                dma((2, ngx)), dma((2, ngx)), dma((2, ngy)), dma((2, ngy)),
            ],
            compiler_params=pltpu.CompilerParams(
                collective_id=0, has_side_effects=True, vmem_limit_bytes=40 * 1024 * 1024),
        )(modes_start, search_start, stiffness, density)
        return modes, search, ritz[0, 0:MODES]

    return jax.shard_map(
        on_device, mesh=mesh,
        in_specs=(P(None, "gx", "gy"), P(None, "gx", "gy"), P("gx", "gy"), P("gx", "gy")),
        out_specs=(P(None, "gx", "gy"), P(None, "gx", "gy"), P()),
        check_vma=False,
    )
```
